32 devices in a mesh: seq: 2 (over y), expert: 16 (over z, x, core).
Axes of the slice: x: 2, y: 2, z: 4, core: 2. Of those that a mesh axis runs over, the one named last changes fastest.
Arguments:
- tokens: bfloat16 [4096, 2048], P(('seq', 'expert')), may hold values from -4 to 4
- routes: int32 [4096, 8], P(('seq', 'expert')), may hold values from 0 to 31, all different within a row; in each aligned block of 128 rows (0 to 127, 128 to 255, ...) at most 64 rows name the same one
- gate_shares: int32 [4096, 8], P(('seq', 'expert')), may hold values from 1 to 65536
- gate_up: bfloat16 [32, 2048, 768], P('expert', 'seq'), may hold values from -0.125 to 0.125
Outputs:
- gram: float32 [32, 384, 384], P('expert', 'seq')
- maxima: float32 [32, 2048], P('expert', 'seq')
The draws below stay inside these ranges and needn't reach their ends.
Inputs may be any that keep to these rules, and one draw needn't show every extreme that they name: `routes`: among the 128 rows of one device no expert is named more than 64 times.
All inputs are finite; a program needn't handle non-finite values.
Results may differ from the reference program's by a relative error of at most 0.0049.
Values may be sent and summed in bfloat16 or wider, within the bound.
No kernel may reach another device: no remote copies, remote signals or barrier semaphores. Data moves between devices by JAX's collectives and lax.ppermute only.
A program may use at most 64 MiB of HBM per device.

```python
import math
import jax
import jax.numpy as jnp
import numpy as np
from jax import lax

D = 2048
FWIN = 384
TOP = 8
TOK_DEV = 128
EXPERTS = 32
CAP = 64
TOKENS = 4096
N_SEQ = 2
N_EXPERT = 16


def draw_tokens(key, part):
    key_base, key_chan, key_row = jax.random.split(key, 3)
    channel_scale = jnp.exp(jax.random.uniform(key_chan, (D,), jnp.float32, -1.15, 1.15))
    row_scale = jnp.exp(jax.random.uniform(key_row, (TOKENS, 1), jnp.float32, -0.5, 0.5))
    base = jax.random.normal(key_base, (TOKENS, D), jnp.float32)
    values = jnp.clip(0.5 * base * channel_scale * row_scale, -4.0, 4.0)
    return values.astype(jnp.bfloat16)


def touch_ends(array, rng, low, high):
    spot = [jax.random.randint(jax.random.fold_in(rng, axis), (), 0, length) for axis, length in enumerate(array.shape)]
    main_axis = array.shape.index(max(array.shape))
    next_to = spot[:main_axis] + [(spot[main_axis] + 1) % array.shape[main_axis]] + spot[main_axis + 1:]
    return array.at[tuple(spot)].set(low).at[tuple(next_to)].set(high)


def level_of(key, extent, cuts, least, top_value):
    factor_of = 1.0
    for position, blocks in cuts:
        heights = jax.random.uniform(jax.random.fold_in(jax.random.fold_in(key, 6), position), (blocks,), jnp.float32, least / len(cuts), top_value / len(cuts))
        factor_of = factor_of * jnp.repeat(jnp.exp(heights), extent[position] // blocks).reshape((-1,) + (1,) * (len(extent) - 1 - position))
    return factor_of


def shared_out(rng, own, number, rows, count, top, most, lean):
    order = jax.random.permutation(rng, count)
    packed, common = portions_of(count, rows * top, most, lean, True), portions_of(count, rows * top, most, lean, False)
    places = jnp.arange(count)

    def named(sizes, offset_by):
        used = int((sizes > 0).sum())
        fixed = max(1, used // 4)
        moved = fixed + (places - fixed + offset_by * (used - fixed)) % max(1, count - fixed)
        return jnp.zeros((count,), jnp.int32).at[order[jnp.where(places < fixed, places, moved)]].set(jnp.asarray(sizes, jnp.int32))

    sizes = jnp.where(number % 4 == 0, named(packed, number // 4), named(common, number - number // 4 - 1))
    mixed = jax.random.permutation(jax.random.fold_in(own, 3), count)
    donor, sink = mixed[0:count // 2 * 2:2], mixed[1:count // 2 * 2:2]
    room = jnp.minimum(sizes[donor] - 1, most - sizes[sink]) // 2
    room = jnp.where((donor == order[0]) | (sink == order[0]) | (sizes[sink] == 0), 0, jnp.maximum(room, 0))
    moved = jax.random.randint(jax.random.fold_in(own, 4), (count // 2,), 0, 1 << 20) % (room + 1)
    sizes = sizes.at[donor].add(-moved).at[sink].add(moved)
    members = jnp.searchsorted(jnp.cumsum(sizes), jnp.arange(rows * top), side="right").astype(jnp.int32)
    listing = members.reshape(top, rows).T
    listing = listing[jax.random.permutation(jax.random.fold_in(own, 1), rows)]
    offset_by = jax.random.randint(jax.random.fold_in(own, 2), (rows, 1), 0, top)
    return jnp.take_along_axis(listing, (jnp.arange(top)[None, :] + offset_by) % top, axis=1)


def portions_of(number_of, total, bound, slope, full):
    portions = [(1 << 20) // math.isqrt(rank ** slope) + 1 for rank in range(1, number_of + 1)]
    largest = bound if full else min(bound, max(-(-total // number_of), total * portions[0] // sum(portions)))
    least = 1 if total - largest >= number_of - 1 else 0
    counts, rest = [largest] + [least] * (number_of - 1), total - largest - least * (number_of - 1)
    while rest > 0:
        candidates = [i for i in range(1, number_of) if counts[i] < largest] or [i for i in range(1, number_of) if counts[i] < bound]
        whole, left = sum([portions[i] for i in candidates]), rest
        for i in candidates:
            more = min(bound - counts[i], max(1, left * portions[i] // whole), rest)
            counts[i] = counts[i] + more
            rest = rest - more
    return np.array(counts)


def noise(stream_key, dims, scale, bound, pieces=(), held_as=jnp.bfloat16):
    drawn = jax.random.normal(stream_key, dims, jnp.float32) * scale
    if len(pieces) > 0:
        drawn = level_of(stream_key, dims, pieces, -0.22, 0.18) * drawn
    return jnp.clip(drawn, min=-bound, max=bound).astype(held_as)


def setup_inputs(seed: int = 0) -> dict:
    streams_of = jax.random.split(jax.random.key(seed), 5)
    tokens = draw_tokens(jax.random.fold_in(streams_of[4], 71), 0)
    routes_keys = jax.random.split(jax.random.fold_in(streams_of[1], 1), TOKENS // TOK_DEV)
    routes_turns = jax.random.permutation(jax.random.fold_in(streams_of[1], 3), TOKENS // TOK_DEV)
    routes = jax.vmap(lambda own, number: shared_out(jax.random.fold_in(streams_of[1], 2), own, number, TOK_DEV, EXPERTS, TOP, CAP, 1))(routes_keys, routes_turns).reshape((TOKENS, TOP))
    gate_shares = touch_ends(jax.random.randint(streams_of[2], (TOKENS, TOP), 1, 65537), jax.random.fold_in(streams_of[2], 1), 1, 65536).astype(jnp.int32)
    gate_up = noise(streams_of[3], (EXPERTS, D, 2 * FWIN), D ** -0.5, 0.125, ((0, 16), (1, 2)))
    return dict(tokens=tokens, routes=routes, gate_shares=gate_shares, gate_up=gate_up)


def reference(tokens, routes, gate_shares, gate_up):
    chosen = routes.reshape(-1).astype(jnp.int32)
    shares = gate_shares.reshape(-1).astype(jnp.float32) / 65536.0
    ordering = jnp.argsort(chosen, stable=True).astype(jnp.int32)
    per_expert = jnp.bincount(chosen, length=EXPERTS).astype(jnp.int32)
    first_slot = (jnp.cumsum(per_expert) - per_expert).astype(jnp.int32)
    longest = N_SEQ * N_EXPERT * CAP
    padded_order = jnp.concatenate([ordering, jnp.zeros((longest,), jnp.int32)])
    norm_factor = EXPERTS / (TOKENS * TOP)

    def expert_stats(expert):
        pair_index = lax.dynamic_slice_in_dim(padded_order, first_slot[expert], longest)
        is_live = jnp.arange(longest, dtype=jnp.int32) < per_expert[expert]
        token_index = (pair_index // TOP).astype(jnp.int32)
        gathered = tokens[token_index]
        channel_max = jnp.max(jnp.where(is_live[:, None], jnp.abs(gathered), 0), axis=0).astype(jnp.float32)
        projected = jnp.dot(gathered, gate_up[expert], preferred_element_type=jnp.float32)
        hidden = (jax.nn.silu(projected[:, :FWIN]) * projected[:, FWIN:]).astype(jnp.bfloat16)
        pair_share = jnp.where(is_live, shares[pair_index], 0.0)
        weighted = hidden.astype(jnp.float32) * pair_share[:, None]
        weighted_high = weighted.astype(jnp.bfloat16)
        weighted_low = (weighted - weighted_high.astype(jnp.float32)).astype(jnp.bfloat16)
        gram_full = jnp.dot(hidden.T, weighted_high, preferred_element_type=jnp.float32)
        gram_full = gram_full + jnp.dot(hidden.T, weighted_low, preferred_element_type=jnp.float32)
        return gram_full * norm_factor, channel_max

    gram, maxima = lax.map(expert_stats, jnp.arange(EXPERTS, dtype=jnp.int32))
    return gram, maxima
```

```python
import functools

import jax
import jax.numpy as jnp
from jax import lax
from jax.experimental import pallas as pl
from jax.experimental.pallas import tpu as pltpu
from jax.sharding import PartitionSpec as P

VMEM_LIMIT = 48 * 1024 * 1024
VM = pl.BlockSpec(memory_space=pltpu.VMEM)
SM = pl.BlockSpec(memory_space=pltpu.SMEM)


def params():
    return pltpu.CompilerParams(vmem_limit_bytes=VMEM_LIMIT)


def cost(flops, moved):
    return pl.CostEstimate(flops=int(flops), bytes_accessed=int(moved), transcendentals=0)


def pack_kernel(experts, tok_ref, routes_ref, shares_ref, out_ref):
    rows, width = tok_ref.shape
    extra = out_ref.shape[1] - width
    out_ref[:, :width] = tok_ref[...]
    lane = lax.broadcasted_iota(jnp.int32, (rows, extra), 1)
    expert = jnp.where(lane < experts, lane, lane - experts)
    value = jnp.zeros((rows, extra), jnp.int32)
    for k in range(routes_ref.shape[1]):
        value = value + jnp.where(routes_ref[:, k : k + 1] == expert, shares_ref[:, k : k + 1], 0)
    share = value.astype(jnp.float32) / 65536.0
    high = share.astype(jnp.bfloat16).astype(jnp.float32)
    low = share - high
    out_ref[:, width:] = jnp.where(lane < experts, high, low).astype(jnp.bfloat16)


def rows_kernel(experts, cap, count, *refs):
    where_ref, w_ref = refs[0], refs[1]
    blocks = refs[2 : 2 + count]
    x_ref, share_ref, p_ref, max_ref = refs[2 + count :]
    local, depth, _ = w_ref.shape
    width = x_ref.shape[2]
    rows = blocks[0].shape[0]
    extra = blocks[0].shape[1] - width
    first = where_ref[0] * local
    lane = lax.broadcasted_iota(jnp.int32, (1, extra), 1)
    slot = lax.broadcasted_iota(jnp.int32, (1, cap), 1).astype(jnp.float32)
    below = (
        lax.broadcasted_iota(jnp.int32, (rows, rows), 0)
        > lax.broadcasted_iota(jnp.int32, (rows, rows), 1)
    ).astype(jnp.bfloat16)
    largest = [jnp.zeros((1, width), jnp.float32) for _ in range(local)]
    for b, block in enumerate(blocks):
        side = block[:, width:].astype(jnp.float32)
        live = jnp.where((side > 0.0) & (lane < experts), 1.0, 0.0)
        rank = jnp.dot(below, live.astype(jnp.bfloat16), preferred_element_type=jnp.float32)
        place = jnp.where(live > 0.0, rank, -1.0)
        picks = []
        for i in range(local):
            mine = jnp.sum(jnp.where(lane == first + i, place, 0.0), axis=1, keepdims=True)
            picks.append(jnp.where(mine == slot, 1.0, 0.0))
        pick = jnp.concatenate(picks, axis=1).astype(jnp.bfloat16)
        taken = lax.dot_general(
            pick, block[...], (((0,), (0,)), ((), ())), preferred_element_type=jnp.float32
        )
        for i in range(local):
            part = taken[i * cap : (i + 1) * cap]
            x_ref[i, b * cap : (b + 1) * cap, :] = part[:, :width].astype(jnp.bfloat16)
            both = (lane == first + i) | (lane == experts + first + i)
            share = jnp.sum(jnp.where(both, part[:, width:], 0.0), axis=1, keepdims=True)
            share_ref[i, b * cap : (b + 1) * cap, :] = jnp.broadcast_to(share, (cap, 128))
            largest[i] = jnp.maximum(
                largest[i], jnp.max(jnp.abs(part[:, :width]), axis=0, keepdims=True)
            )
    for i in range(local):
        max_ref[i : i + 1, :] = largest[i]
    start = pl.multiple_of(where_ref[1] * depth, 128)
    for i in range(local):
        p_ref[i] = jnp.dot(
            x_ref[i, :, pl.ds(start, depth)], w_ref[i], preferred_element_type=jnp.float32
        )


def rows_of(experts, cap, where, weights, blocks):
    count, local, depth, fan = len(blocks), *weights.shape
    rows, full = blocks[0].shape
    width = 2 * depth
    total = count * cap
    return pl.pallas_call(
        functools.partial(rows_kernel, experts, cap, count),
        out_shape=(
            jax.ShapeDtypeStruct((local, total, width), jnp.bfloat16),
            jax.ShapeDtypeStruct((local, total, 128), jnp.float32),
            jax.ShapeDtypeStruct((local, total, fan), jnp.float32),
            jax.ShapeDtypeStruct((local, width), jnp.float32),
        ),
        in_specs=[SM] + [VM] * (1 + count),
        out_specs=(VM,) * 4,
        compiler_params=params(),
        cost_estimate=cost(
            2 * local * total * depth * fan + 2 * count * rows * local * cap * full,
            2 * count * rows * full + 2 * local * depth * fan + local * total * (2 * width + 4 * fan),
        ),
        name="expert_rows",
    )(where, weights, *blocks)


def more_kernel(offset, where_ref, w_ref, x_ref, p_ref, out_ref):
    depth = w_ref.shape[0]
    half = x_ref.shape[2] // 2
    start = pl.multiple_of((1 - where_ref[1]) * half + offset, 128)
    out_ref[0] = p_ref[0] + jnp.dot(
        x_ref[0, :, pl.ds(start, depth)], w_ref[...], preferred_element_type=jnp.float32
    )


def expert_spec(array, expert):
    return pl.BlockSpec((1,) + array.shape[1:], lambda g, e=expert: (e, 0, 0))


def more_of(where, weights, x, p, expert, offset):
    rows, fan = p.shape[1:]
    depth = weights.shape[0]
    return pl.pallas_call(
        functools.partial(more_kernel, offset),
        grid=(1,),
        out_shape=jax.ShapeDtypeStruct((1, rows, fan), jnp.float32),
        in_specs=[
            SM,
            pl.BlockSpec(weights.shape, lambda g: (0, 0)),
            expert_spec(x, expert),
            expert_spec(p, expert),
        ],
        out_specs=pl.BlockSpec((1, rows, fan), lambda g: (0, 0, 0)),
        compiler_params=params(),
        cost_estimate=cost(2 * rows * depth * fan, 8 * rows * fan + 2 * rows * x.shape[2]),
        name="more_terms",
    )(where, weights, x, p)


def gram_kernel(offsets, groups, carried, last, factor, *refs):
    where_ref = refs[0]
    w_refs = refs[1 : 1 + len(offsets)]
    ins = refs[1 + len(offsets) :]
    fan = w_refs[0].shape[1]
    wide = fan // 2
    total = None
    for g in range(groups):
        x_ref, share_ref, p_ref = ins[3 * g : 3 * g + 3]
        half = x_ref.shape[2] // 2
        value = p_ref[0]
        for offset, w_ref in zip(offsets, w_refs):
            start = pl.multiple_of((1 - where_ref[1]) * half + offset, 128)
            value = value + jnp.dot(
                x_ref[0, :, pl.ds(start, w_ref.shape[0])],
                w_ref[...],
                preferred_element_type=jnp.float32,
            )
        gate = value[:, :wide]
        hidden = (gate / (1.0 + jnp.exp(-gate)) * value[:, wide:]).astype(jnp.bfloat16)
        weighted = hidden.astype(jnp.float32) * share_ref[0, :, 0:1]
        high = weighted.astype(jnp.bfloat16)
        low = (weighted - high.astype(jnp.float32)).astype(jnp.bfloat16)
        dims = (((0,), (0,)), ((), ()))
        term = lax.dot_general(hidden, high, dims, preferred_element_type=jnp.float32)
        term = term + lax.dot_general(hidden, low, dims, preferred_element_type=jnp.float32)
        total = term if total is None else total + term
    rest = ins[3 * groups :]
    if carried:
        total = total + rest[0][...]
        rest = rest[1:]
    if not last:
        rest[0][...] = total
        return
    own_ref, send_ref, hold_ref = rest
    hold_ref[...] = total * factor
    part = own_ref.shape[0]
    own_ref[...] = hold_ref[pl.ds(pl.multiple_of(where_ref[1] * part, 16), part), :]
    send_ref[...] = hold_ref[pl.ds(pl.multiple_of((1 - where_ref[1]) * part, 16), part), :].astype(
        jnp.bfloat16
    )


def gram_of(where, weights, offsets, groups, expert, carried, last, factor):
    fan = weights[0].shape[1]
    wide = fan // 2
    ins, specs, rows = [], [], 0
    for x, share, p, place in groups:
        ins += [x, share, p]
        specs += [expert_spec(x, expert), expert_spec(share, expert), expert_spec(p, place)]
        rows += x.shape[1]
    whole = pl.BlockSpec((wide, wide), lambda g: (0, 0))
    if carried is not None:
        ins.append(carried)
        specs.append(whole)
    if last:
        piece = pl.BlockSpec((wide // 2, wide), lambda g: (0, 0))
        out_shape = (
            jax.ShapeDtypeStruct((wide // 2, wide), jnp.float32),
            jax.ShapeDtypeStruct((wide // 2, wide), jnp.bfloat16),
        )
        out_specs = (piece, piece)
        scratch = [pltpu.VMEM((wide, wide), jnp.float32)]
    else:
        out_shape = jax.ShapeDtypeStruct((wide, wide), jnp.float32)
        out_specs = whole
        scratch = []
    depth = sum(w.shape[0] for w in weights)
    return pl.pallas_call(
        functools.partial(
            gram_kernel, offsets, len(groups), carried is not None, last, factor
        ),
        grid=(1,),
        out_shape=out_shape,
        in_specs=[SM] + [pl.BlockSpec(w.shape, lambda g: (0, 0)) for w in weights] + specs,
        out_specs=out_specs,
        scratch_shapes=scratch,
        compiler_params=params(),
        cost_estimate=cost(
            2 * rows * (depth * fan + 2 * wide * wide), rows * (4 * fan + 4 * depth) + 2 * depth * fan
        ),
        name="expert_gram",
    )(where, *weights, *ins)


def tie(*arrays):
    return lax.optimization_barrier(arrays)


def gather_body(capacity, tokens, routes, gate_shares, gate_up):
    tok_rows, width = tokens.shape
    top_count = routes.shape[1]
    expert_count = lax.axis_size("expert")
    seq_count = lax.axis_size("seq")
    local_count, depth, _ = gate_up.shape
    all_experts = local_count * expert_count
    factor = all_experts / (tok_rows * seq_count * expert_count * top_count)
    columns = expert_count // 4

    def moved(array, target):
        places = [(z, x, c) for z in range(columns) for x in range(2) for c in range(2)]
        number = {place: n for n, place in enumerate(places)}
        return lax.ppermute(array, "expert", [(number[p], number[target(*p)]) for p in places])

    def along_z(array, k):
        return moved(array, lambda z, x, c: ((z + k) % columns, x, c))

    def along_x(array):
        return moved(array, lambda z, x, c: (z, 1 - x, c))

    def along_core(array):
        return moved(array, lambda z, x, c: (z, x, 1 - c))

    def swapped(array):
        return lax.ppermute(array, "seq", [(0, 1), (1, 0)])

    where = jnp.stack([lax.axis_index("expert"), lax.axis_index("seq")]).astype(jnp.int32)
    extra = -(-2 * all_experts // 128) * 128
    own = pl.pallas_call(
        functools.partial(pack_kernel, all_experts),
        out_shape=jax.ShapeDtypeStruct((tok_rows, width + extra), jnp.bfloat16),
        in_specs=[VM] * 3,
        out_specs=VM,
        compiler_params=params(),
        cost_estimate=cost(0, 4 * tok_rows * width),
        name="packed_tokens",
    )(tokens, routes, gate_shares)
    rows_from = functools.partial(rows_of, all_experts, capacity, where, gate_up)

    cut = depth // 2
    w00 = swapped(gate_up[0, :cut])
    w01 = swapped(gate_up[0, cut:])
    z1 = along_z(own, 1)
    x0 = along_x(own)
    z3 = along_z(own, columns - 1)
    c0 = along_core(own)
    x0, c0 = tie(x0, c0)
    cx0 = along_core(x0)
    own2, z1, z3, cx0, x0, c0, w00, w1a, w1b = tie(
        own, z1, z3, cx0, x0, c0, w00, gate_up[1, :cut], gate_up[1, cut:]
    )
    w10 = swapped(w1a)
    z2 = along_z(own2, 2)
    x1, x3, c1, c3 = along_x(z1), along_x(z3), along_core(z1), along_core(z3)
    g0 = rows_from((own2, c0, x0, cx0))
    z2, x1, x3, c1, c3, w01, w1b, *g0 = tie(z2, x1, x3, c1, c3, w01, w1b, *g0)
    w11 = swapped(w1b)
    x2, c2, cx1, cx3 = along_x(z2), along_core(z2), along_core(x1), along_core(x3)
    g1 = rows_from((z1, c1, x1, cx1, z3, c3, x3, cx3))
    e0 = gram_of(
        where, (w00, w01), (0, cut), [(g[0], g[1], g[2], 0) for g in (g0, g1)], 0, None, False, factor
    )
    x2, e0, *g1 = tie(x2, e0, *g1)
    cx2 = along_core(x2)
    p1 = [more_of(where, w10, g[0], g[2], 1, 0) for g in (g0, g1)]
    cx2, *p1 = tie(cx2, *p1)
    g2 = rows_from((z2, c2, x2, cx2))
    own0, send0 = gram_of(
        where, (w00, w01), (0, cut), [(g2[0], g2[1], g2[2], 0)], 0, e0, True, factor
    )
    p1.append(more_of(where, w10, g2[0], g2[2], 1, 0))
    got0 = swapped(send0)
    largest = functools.reduce(jnp.maximum, [g[3] for g in (g0, g1, g2)])
    mine = lax.axis_index("seq")
    keep = lax.dynamic_slice_in_dim(largest, mine * depth, depth, 1)
    give = lax.dynamic_slice_in_dim(largest, (1 - mine) * depth, depth, 1)
    maxima = jnp.maximum(keep, swapped(give))
    own1, send1 = gram_of(
        where,
        (w11,),
        (cut,),
        [(g[0], g[1], p, 0) for g, p in zip((g0, g1, g2), p1)],
        1,
        None,
        True,
        factor,
    )
    got1 = swapped(send1)
    gram = jnp.stack([own0 + got0.astype(jnp.float32), own1 + got1.astype(jnp.float32)])
    return (gram, maxima)


def routed_body(capacity, tokens, routes, gate_shares, gate_up):
    tok_rows, width = tokens.shape
    top_count = routes.shape[1]
    expert_count = lax.axis_size("expert")
    seq_count = lax.axis_size("seq")
    local_count, _, fan = gate_up.shape
    wide = fan // 2
    all_experts = local_count * expert_count
    norm_factor = all_experts / (tok_rows * seq_count * expert_count * top_count)
    chosen = routes.reshape(-1)
    shares = gate_shares.reshape(-1).astype(jnp.float32) / 65536.0
    one_hot = (chosen[:, None] == jnp.arange(all_experts, dtype=jnp.int32)[None, :]).astype(jnp.int32)
    ranked = jnp.sum((jnp.cumsum(one_hot, axis=0) - one_hot) * one_hot, axis=1)
    slot_index = chosen * capacity + ranked
    token_index = jnp.arange(tok_rows * top_count, dtype=jnp.int32) // top_count
    outgoing = (
        jnp.zeros((all_experts * capacity, width), jnp.bfloat16)
        .at[slot_index]
        .set(tokens[token_index])
        .reshape(expert_count, local_count, capacity, width)
    )
    out_shares = (
        jnp.zeros((all_experts * capacity,), jnp.float32)
        .at[slot_index]
        .set(shares)
        .reshape(expert_count, local_count, capacity)
    )
    arrived = lax.all_to_all(outgoing, "expert", split_axis=0, concat_axis=0, tiled=True)
    arrived_shares = lax.all_to_all(out_shares, "expert", split_axis=0, concat_axis=0, tiled=True)
    channel_max = jnp.max(
        jnp.where(arrived_shares[..., None] > 0.0, jnp.abs(arrived), 0), axis=(0, 2)
    ).astype(jnp.float32)
    projected = jnp.einsum(
        "slcd,ldf->lscf",
        arrived,
        lax.all_gather(gate_up, "seq", axis=1, tiled=True),
        preferred_element_type=jnp.float32,
    )
    hidden = (jax.nn.silu(projected[..., :wide]) * projected[..., wide:]).astype(jnp.bfloat16)
    hidden = hidden.reshape(local_count, expert_count * capacity, wide)
    row_shares = jnp.transpose(arrived_shares, (1, 0, 2)).reshape(local_count, -1)
    weighted = hidden.astype(jnp.float32) * row_shares[..., None]
    high = weighted.astype(jnp.bfloat16)
    low = (weighted - high.astype(jnp.float32)).astype(jnp.bfloat16)
    gram = jnp.einsum("lrf,lrg->lfg", hidden, high, preferred_element_type=jnp.float32)
    gram = gram + jnp.einsum("lrf,lrg->lfg", hidden, low, preferred_element_type=jnp.float32)
    gram = lax.psum_scatter(gram * norm_factor, "seq", scatter_dimension=1, tiled=True)
    full_max = lax.pmax(channel_max, "seq")
    part = width // seq_count
    maxima = lax.dynamic_slice_in_dim(full_max, lax.axis_index("seq") * part, part, 1)
    return (gram, maxima)


def body(tokens, routes, gate_shares, gate_up):
    expert_count = lax.axis_size("expert")
    local_count = gate_up.shape[0]
    rows = tokens.shape[0]
    capacity = 2 * rows * routes.shape[1] // (local_count * expert_count)
    whole_rows = rows <= local_count * capacity
    shaped = lax.axis_size("seq") == 2 and expert_count == 16 and local_count == 2
    plan = gather_body if whole_rows and shaped else routed_body
    return plan(capacity, tokens, routes, gate_shares, gate_up)


def solution(mesh):
    return jax.shard_map(
        body,
        mesh=mesh,
        in_specs=(
            P(("seq", "expert"), None),
            P(("seq", "expert"), None),
            P(("seq", "expert"), None),
            P("expert", "seq", None),
        ),
        out_specs=(P("expert", "seq", None), P("expert", "seq")),
        check_vma=False,
    )
```

```python
import functools
import math

import jax
import jax.numpy as jnp
from jax import lax
from jax.experimental import pallas as pl
from jax.experimental.pallas import tpu as pltpu
from jax.sharding import PartitionSpec as P

VMEM_LIMIT = 18 * 1024 * 1024
FIRST_LIMIT = 60 * 1024 * 1024
VM = pl.BlockSpec(memory_space=pltpu.VMEM)
SM = pl.BlockSpec(memory_space=pltpu.SMEM)


def params(limit=VMEM_LIMIT):
    return pltpu.CompilerParams(vmem_limit_bytes=limit)


def cost(flops, moved):
    return pl.CostEstimate(flops=16 * int(flops), bytes_accessed=16 * int(moved), transcendentals=0)


def pack_kernel(experts, tok_ref, routes_ref, shares_ref, w_ref, out_ref, piece_ref, small_ref, sems):
    rows, width = tok_ref.shape
    top = routes_ref.shape[0]
    extra = out_ref.shape[1] - width
    copies = [
        pltpu.make_async_copy(source, target, sems.at[k])
        for k, (source, target) in enumerate(
            (
                (routes_ref, small_ref.at[0]),
                (shares_ref, small_ref.at[1]),
                (tok_ref, out_ref.at[:, pl.ds(0, width)]),
                (w_ref.at[pl.ds(0, piece_ref.shape[0]), :], piece_ref),
            )
        )
    ]
    for copy in copies:
        copy.start()
    copies[0].wait()
    copies[1].wait()
    routes, shares = small_ref[0].T, small_ref[1].T
    lane = lax.broadcasted_iota(jnp.int32, (rows, extra), 1)
    expert = jnp.where(lane < experts, lane, lane - experts)
    value = jnp.zeros((rows, extra), jnp.int32)
    for k in range(top):
        value = value + jnp.where(routes[:, k : k + 1] == expert, shares[:, k : k + 1], 0)
    share = value.astype(jnp.float32) / 65536.0
    high = share.astype(jnp.bfloat16).astype(jnp.float32)
    low = share - high
    out_ref[:, width:] = jnp.where(lane < experts, high, low).astype(jnp.bfloat16)
    copies[2].wait()
    copies[3].wait()


def pick_kernel(experts, cap, count, *refs):
    where_ref = refs[0]
    blocks = refs[1 : 1 + count]
    own_ref, other_ref = refs[1 + count :]
    rows, full = blocks[0].shape
    local = own_ref.shape[0] // (count * cap)
    extra = -(-2 * experts // 128) * 128
    width = full - extra
    lane = lax.broadcasted_iota(jnp.int32, (1, extra), 1)
    slot = lax.broadcasted_iota(jnp.int32, (1, cap), 1).astype(jnp.float32)
    below = (
        lax.broadcasted_iota(jnp.int32, (rows, rows), 0)
        > lax.broadcasted_iota(jnp.int32, (rows, rows), 1)
    ).astype(jnp.bfloat16)
    firsts = (where_ref[0] * local, where_ref[1] * local)
    lives = []
    for block in blocks:
        side = block[:, width:].astype(jnp.float32)
        lives.append(jnp.where((side > 0.0) & (lane < experts), 1.0, 0.0))
    live = jnp.concatenate(lives, axis=1)
    rank = jnp.dot(below, live.astype(jnp.bfloat16), preferred_element_type=jnp.float32)
    place = jnp.where(live > 0.0, rank, -1.0)
    picks = []
    for b in range(count):
        at = place[:, b * extra : (b + 1) * extra]
        mine = [
            jnp.sum(jnp.where(lane == first + i, at, 0.0), axis=1, keepdims=True)
            for first in firsts
            for i in range(local)
        ]
        pick = jnp.concatenate([jnp.where(m == slot, 1.0, 0.0) for m in mine], axis=1)
        picks.append(pick.astype(jnp.bfloat16))
    for b, block in enumerate(blocks):
        taken = lax.dot_general(
            picks[b], block[...], (((0,), (0,)), ((), ())), preferred_element_type=jnp.float32
        ).astype(jnp.bfloat16)
        for k, ref in enumerate((own_ref, other_ref)):
            for i in range(local):
                at = (i * count + b) * cap
                got = (k * local + i) * cap
                ref[at : at + cap, :] = taken[got : got + cap]


def picked(experts, cap, local, where, blocks):
    count = len(blocks)
    rows, full = blocks[0].shape
    out = jax.ShapeDtypeStruct((local * count * cap, full), jnp.bfloat16)
    return pl.pallas_call(
        functools.partial(pick_kernel, experts, cap, count),
        out_shape=(out, out),
        in_specs=[SM] + [VM] * count,
        out_specs=(VM, VM),
        compiler_params=params(),
        cost_estimate=cost(
            4 * count * rows * local * cap * full, 2 * count * full * (rows + 2 * local * cap)
        ),
        name="picked_rows",
    )(where, *blocks)


def hidden_terms(value, share):
    wide = value.shape[1] // 2
    gate = value[:, :wide]
    hidden = (gate / (1.0 + jnp.exp(-gate)) * value[:, wide:]).astype(jnp.bfloat16)
    weighted = hidden.astype(jnp.float32) * share
    high = weighted.astype(jnp.bfloat16)
    low = (weighted - high.astype(jnp.float32)).astype(jnp.bfloat16)
    return hidden, high, low


def gram_terms(hidden_ref, weighted_ref):
    wide = hidden_ref.shape[1]
    both = lax.dot_general(
        hidden_ref[...],
        weighted_ref[...],
        (((0,), (0,)), ((), ())),
        preferred_element_type=jnp.float32,
    )
    return both[:, :wide] + both[:, wide:]


def hidden_and_gram(value, share, hidden_ref, weighted_ref):
    wide = hidden_ref.shape[1]
    hidden_ref[...], weighted_ref[:, :wide], weighted_ref[:, wide:] = hidden_terms(value, share)
    return gram_terms(hidden_ref, weighted_ref)


def give_out(total, seq, own_ref, send_ref, hold_ref):
    hold_ref[...] = total
    part = own_ref.shape[0]
    own_ref[...] = hold_ref[pl.ds(pl.multiple_of(seq * part, 16), part), :]
    send_ref[...] = hold_ref[pl.ds(pl.multiple_of((1 - seq) * part, 16), part), :].astype(
        jnp.bfloat16
    )


def experts_kernel(experts, pieces, count, carried, final, factor, *refs):
    where_ref, w_ref = refs[:2]
    far_refs = refs[2 : 2 + pieces]
    groups = refs[2 + pieces : 2 + pieces + count]
    rest = refs[2 + pieces + count :]
    if carried:
        gram_in_ref, max_in_ref = rest[:2]
        rest = rest[2:]
    max_ref, p_ref, late_ref = rest[:3]
    hidden_ref, weighted_ref = rest[-2:]
    rest = rest[3:-2]
    local, depth, fan = w_ref.shape
    extra = -(-2 * experts // 128) * 128
    width = groups[0].shape[1] - extra
    lane = lax.broadcasted_iota(jnp.int32, (1, extra), 1)
    first, seq = where_ref[0] * local, where_ref[2]
    near, far = pl.multiple_of(seq * depth, 128), pl.multiple_of((1 - seq) * depth, 128)

    def part(i, columns):
        each = [g.shape[0] // local for g in groups]
        return jnp.concatenate(
            [g[i * n : (i + 1) * n, columns] for g, n in zip(groups, each)], axis=0
        )

    def share_of(i):
        both = (lane == first + i) | (lane == experts + first + i)
        side = part(i, slice(width, width + extra)).astype(jnp.float32)
        return jnp.sum(jnp.where(both, side, 0.0), axis=1, keepdims=True)

    def product(a, w):
        return jnp.dot(a, w, preferred_element_type=jnp.float32)

    values = [product(part(i, pl.ds(near, depth)), w_ref[i]) for i in range(local)]
    at = 0
    for far_ref in far_refs:
        end = at + far_ref.shape[0]
        for i in range(local):
            low, high = max(at, i * depth), min(end, (i + 1) * depth)
            if low < high:
                columns = pl.ds(pl.multiple_of(far + low - i * depth, 128), high - low)
                values[i] = values[i] + product(part(i, columns), far_ref[low - at : high - at, :])
        at = end
    known = at - depth
    total = hidden_and_gram(values[0], share_of(0), hidden_ref, weighted_ref)
    p_ref[:, :fan] = values[1]
    p_ref[:, fan:] = jnp.broadcast_to(share_of(1), (p_ref.shape[0], 128))
    late_ref[...] = part(1, pl.ds(pl.multiple_of(far + known, 128), depth - known))
    for i in range(local):
        size = jnp.abs(part(i, slice(0, width)))
        largest = max_in_ref[i * 16 : (i + 1) * 16, :] if carried else size[:16]
        for r in range(0 if carried else 16, size.shape[0], 16):
            largest = jnp.maximum(largest, size[r : r + 16])
        max_ref[i * 16 : (i + 1) * 16, :] = largest
    if carried:
        total = total + gram_in_ref[...]
    if final:
        give_out(total * factor, seq, *rest)
    else:
        rest[0][...] = total


def experts_of(experts, where, weights, far, groups, carried, final, factor):
    local, depth, fan = weights.shape
    wide = fan // 2
    rows = sum(g.shape[0] for g in groups) // local
    width = 2 * depth
    out = [
        jax.ShapeDtypeStruct((local * 16, width), jnp.bfloat16),
        jax.ShapeDtypeStruct((rows, fan + 128), jnp.float32),
        jax.ShapeDtypeStruct((rows, 2 * depth - depth_of(far)), jnp.bfloat16),
    ]
    scratch = [pltpu.VMEM((rows, wide), jnp.bfloat16), pltpu.VMEM((rows, fan), jnp.bfloat16)]
    if final:
        out += [
            jax.ShapeDtypeStruct((wide // 2, wide), jnp.float32),
            jax.ShapeDtypeStruct((wide // 2, wide), jnp.bfloat16),
        ]
        scratch = [pltpu.VMEM((wide, wide), jnp.float32)] + scratch
    else:
        out.append(jax.ShapeDtypeStruct((wide, wide), jnp.float32))
    ins = [weights, *far, *groups, *(carried or ())]
    return pl.pallas_call(
        functools.partial(experts_kernel, experts, len(far), len(groups), bool(carried), final, factor),
        out_shape=tuple(out),
        in_specs=[SM] + [VM] * len(ins),
        out_specs=(VM,) * len(out),
        scratch_shapes=scratch,
        compiler_params=params(),
        cost_estimate=cost(2 * rows * (depth + depth_of(far)) * fan, 0),
        name="expert_terms",
    )(where, *ins)


def more_kernel(pieces, count, *refs):
    w_refs = refs[:pieces]
    outs = refs[pieces + 2 * count :]
    fan = w_refs[0].shape[1]
    for g in range(count):
        x_ref, p_ref = refs[pieces + 2 * g : pieces + 2 * g + 2]
        value, at = p_ref[:, :fan], 0
        for w_ref in w_refs:
            depth = w_ref.shape[0]
            value = value + jnp.dot(
                x_ref[:, at : at + depth], w_ref[...], preferred_element_type=jnp.float32
            )
            at += depth
        outs[g][:, :fan] = value


def more_of(weights, parts):
    ins = [array for part in parts for array in part]
    return pl.pallas_call(
        functools.partial(more_kernel, len(weights), len(parts)),
        out_shape=tuple(jax.ShapeDtypeStruct(p.shape, p.dtype) for _, p in parts),
        in_specs=[VM] * (len(weights) + len(ins)),
        out_specs=(VM,) * len(parts),
        input_output_aliases={len(weights) + 2 * g + 1: g for g in range(len(parts))},
        compiler_params=params(),
        cost_estimate=cost(
            2 * sum(p.shape[0] for _, p in parts) * depth_of(weights) * weights[0].shape[1], 0
        ),
        name="more_terms",
    )(*weights, *ins)


def last_kernel(step, firsts, factor, *refs):
    where_ref, w_ref = refs[:2]
    count = len(firsts) - 1
    groups = refs[2 : 2 + 2 * count]
    own_ref, send_ref, hold_ref, hidden_ref, weighted_ref = refs[2 + 2 * count :]
    fan = w_ref.shape[1]
    wide = fan // 2
    now = pl.program_id(0)
    for g in range(count):

        @pl.when((now >= firsts[g]) & (now < firsts[g + 1]))
        def _(g=g):
            x_ref, p_ref = groups[2 * g : 2 * g + 2]
            value = p_ref[:, :fan] + jnp.dot(
                x_ref[...], w_ref[...], preferred_element_type=jnp.float32
            )
            hidden, high, low = hidden_terms(value, p_ref[:, fan : fan + 1])
            rows = pl.ds(pl.multiple_of(now * step, step), step)
            hidden_ref[rows, :] = hidden
            weighted_ref[rows, :wide] = high
            weighted_ref[rows, wide:] = low

    @pl.when(now == firsts[-1] - 1)
    def _():
        total = gram_terms(hidden_ref, weighted_ref)
        give_out(total * factor, where_ref[2], own_ref, send_ref, hold_ref)


def last_of(where, weights, parts, factor):
    depth, fan = weights.shape
    wide = fan // 2
    rows = [p.shape[0] for _, p in parts]
    step = functools.reduce(math.gcd, rows, 256)
    firsts = [0]
    ins, specs = [], []
    for x, p in parts:
        first, number = firsts[-1], p.shape[0] // step
        firsts.append(first + number)
        for array, columns in ((x, depth), (p, p.shape[1])):
            ins.append(array)
            specs.append(
                pl.BlockSpec(
                    (step, columns),
                    lambda g, first=first, number=number, at=array.shape[1] // columns - 1: (
                        jnp.clip(g - first, 0, number - 1),
                        at,
                    ),
                )
            )
    return pl.pallas_call(
        functools.partial(last_kernel, step, tuple(firsts), factor),
        grid=(firsts[-1],),
        out_shape=(
            jax.ShapeDtypeStruct((wide // 2, wide), jnp.float32),
            jax.ShapeDtypeStruct((wide // 2, wide), jnp.bfloat16),
        ),
        in_specs=[SM, pl.BlockSpec(weights.shape, lambda g: (0, 0))] + specs,
        out_specs=(pl.BlockSpec((wide // 2, wide), lambda g: (0, 0)),) * 2,
        scratch_shapes=[
            pltpu.VMEM((wide, wide), jnp.float32),
            pltpu.VMEM((sum(rows), wide), jnp.bfloat16),
            pltpu.VMEM((sum(rows), fan), jnp.bfloat16),
        ],
        compiler_params=params(),
        cost_estimate=cost(2 * sum(rows) * depth * fan, 0),
        name="last_terms",
    )(where, weights, *ins)


def depth_of(weights):
    return sum(w.shape[0] for w in weights)


def split_kernel(pieces, w_ref, after_ref, *refs):
    outs, sems = refs[: len(pieces)], refs[len(pieces)]
    copies = [
        pltpu.make_async_copy(w_ref.at[pl.ds(r, n), :], out, sems.at[k])
        for k, ((r, n), out) in enumerate(zip(pieces, outs))
    ]
    for copy in copies:
        copy.start()
    for copy in copies:
        copy.wait()


def split_of(flat, after, pieces):
    anywhere = pl.BlockSpec(memory_space=pl.ANY)
    return pl.pallas_call(
        functools.partial(split_kernel, pieces),
        out_shape=tuple(jax.ShapeDtypeStruct((n, flat.shape[1]), flat.dtype) for _, n in pieces),
        in_specs=[anywhere, anywhere],
        out_specs=(anywhere,) * len(pieces),
        scratch_shapes=[pltpu.SemaphoreType.DMA((len(pieces),))],
        compiler_params=params(),
        cost_estimate=cost(0, 0),
        name="weight_pieces",
    )(flat, after)


def tie(*arrays):
    return lax.optimization_barrier(arrays)


def gather_body(capacity, tokens, routes, gate_shares, gate_up):
    tok_rows, width = tokens.shape
    top_count = routes.shape[1]
    expert_count = lax.axis_size("expert")
    seq_count = lax.axis_size("seq")
    local_count, depth, fan = gate_up.shape
    all_experts = local_count * expert_count
    factor = all_experts / (tok_rows * seq_count * expert_count * top_count)
    columns = expert_count // 4

    def moved(array, target):
        places = [(z, x, c) for z in range(columns) for x in range(2) for c in range(2)]
        number = {place: n for n, place in enumerate(places)}
        return lax.ppermute(array, "expert", [(number[p], number[target(*p)]) for p in places])

    def hop(array, pairs):
        return lax.ppermute(
            array, "expert", [(4 * a + n, 4 * b + n) for a, b in pairs for n in range(4)]
        )

    def along_x(array):
        return moved(array, lambda z, x, c: (z, 1 - x, c))

    def along_core(array):
        return moved(array, lambda z, x, c: (z, x, 1 - c))

    def swapped(array):
        return lax.ppermute(array, "seq", [(0, 1), (1, 0)])

    index, seq = lax.axis_index("expert"), lax.axis_index("seq")
    where = jnp.stack([index, index + 1 - 2 * (index % 2), seq]).astype(jnp.int32)
    extra = -(-2 * all_experts // 128) * 128
    flat = gate_up.reshape(local_count * depth, fan)
    cuts = [depth // 8 * n for n in (0, 8, 11, 14, 16)]
    spans = [(low, high - low) for low, high in zip(cuts, cuts[1:])]
    anywhere = pl.BlockSpec(memory_space=pl.ANY)
    own, piece = pl.pallas_call(
        functools.partial(pack_kernel, all_experts),
        out_shape=(
            jax.ShapeDtypeStruct((tok_rows, width + extra), jnp.bfloat16),
            jax.ShapeDtypeStruct((spans[0][1], fan), jnp.bfloat16),
        ),
        in_specs=[anywhere] * 4,
        out_specs=(VM, VM),
        scratch_shapes=[
            pltpu.VMEM((2, top_count, tok_rows), jnp.int32),
            pltpu.SemaphoreType.DMA((4,)),
        ],
        compiler_params=params(FIRST_LIMIT),
        cost_estimate=cost(0, 4 * tok_rows * width),
        name="packed_tokens",
    )(tokens, routes.T, gate_shares.T, flat)
    far1 = swapped(piece)
    pick = functools.partial(picked, all_experts, capacity, local_count, where)
    terms = functools.partial(experts_of, all_experts, where, gate_up)

    outer = (index // 4 == 0) | (index // 4 == columns - 1)
    za, zm, x0 = hop(own, ((0, 1), (1, 0), (2, 3), (3, 2))), hop(own, ((1, 2), (2, 1))), along_x(own)
    pieces = split_of(flat, own, tuple(spans[1:]))
    own, za, zm, x0, *pieces = tie(own, za, zm, x0, *pieces)
    zo, zi, xa = hop(zm, ((1, 0), (2, 3))), hop(za, ((1, 2), (2, 1))), along_x(za)
    m0, o0 = pick((own, x0))
    zc = jnp.where(outer, zo, zi)
    zc, xa, o0, far1, zm, za, *pieces = tie(zc, xa, o0, far1, zm, za, *pieces)
    zr, xc = hop(zc, ((1, 0), (2, 3))), along_x(zc)
    far2 = swapped(pieces[0])
    r0 = along_core(o0)
    m1, o1 = pick((za, xa))
    zb = jnp.where(outer, zr, zm)
    zb, xc, r0, o1, zc, far2, *pieces = tie(zb, xc, r0, o1, zc, far2, *pieces)
    xb = along_x(zb)
    r1 = along_core(o1)
    far3 = swapped(pieces[1])
    m2, o2 = pick((zc, xc))
    max0, p0, late0, gram0 = terms((far1,), (m0, r0, m1, r1), None, False, factor)
    xb, o2, gram0, max0, far3, zb, *pieces = tie(xb, o2, gram0, max0, far3, zb, *pieces)
    far4 = swapped(pieces[2])
    r2 = along_core(o2)
    m3, o3 = pick((zb, xb))
    r3 = along_core(o3)
    max0, p1, late1, gram0 = terms((far1,), (m2, r2), (gram0, max0), False, factor)
    p0, p1 = more_of((far2, far3), ((late0, p0), (late1, p1)))
    largest, p2, late2, own0, send0 = terms(
        (far1, far2, far3), (m3, r3), (gram0, max0), True, factor
    )
    got0 = swapped(send0)
    largest = jnp.max(largest.reshape(local_count, -1, width), axis=1).astype(jnp.float32)
    keep = lax.dynamic_slice_in_dim(largest, seq * depth, depth, 1)
    give = lax.dynamic_slice_in_dim(largest, (1 - seq) * depth, depth, 1)
    maxima = jnp.maximum(keep, swapped(give))
    own1, send1 = last_of(where, far4, ((late0, p0), (late1, p1), (late2, p2)), factor)
    got1 = swapped(send1)
    gram = jnp.stack([own0 + got0.astype(jnp.float32), own1 + got1.astype(jnp.float32)])
    return (gram, maxima)


def routed_body(capacity, tokens, routes, gate_shares, gate_up):
    tok_rows, width = tokens.shape
    top_count = routes.shape[1]
    expert_count = lax.axis_size("expert")
    seq_count = lax.axis_size("seq")
    local_count, _, fan = gate_up.shape
    wide = fan // 2
    all_experts = local_count * expert_count
    norm_factor = all_experts / (tok_rows * seq_count * expert_count * top_count)
    chosen = routes.reshape(-1)
    shares = gate_shares.reshape(-1).astype(jnp.float32) / 65536.0
    one_hot = (chosen[:, None] == jnp.arange(all_experts, dtype=jnp.int32)[None, :]).astype(jnp.int32)
    ranked = jnp.sum((jnp.cumsum(one_hot, axis=0) - one_hot) * one_hot, axis=1)
    slot_index = chosen * capacity + ranked
    token_index = jnp.arange(tok_rows * top_count, dtype=jnp.int32) // top_count
    outgoing = (
        jnp.zeros((all_experts * capacity, width), jnp.bfloat16)
        .at[slot_index]
        .set(tokens[token_index])
        .reshape(expert_count, local_count, capacity, width)
    )
    out_shares = (
        jnp.zeros((all_experts * capacity,), jnp.float32)
        .at[slot_index]
        .set(shares)
        .reshape(expert_count, local_count, capacity)
    )
    arrived = lax.all_to_all(outgoing, "expert", split_axis=0, concat_axis=0, tiled=True)
    arrived_shares = lax.all_to_all(out_shares, "expert", split_axis=0, concat_axis=0, tiled=True)
    channel_max = jnp.max(
        jnp.where(arrived_shares[..., None] > 0.0, jnp.abs(arrived), 0), axis=(0, 2)
    ).astype(jnp.float32)
    projected = jnp.einsum(
        "slcd,ldf->lscf",
        arrived,
        lax.all_gather(gate_up, "seq", axis=1, tiled=True),
        preferred_element_type=jnp.float32,
    )
    hidden = (jax.nn.silu(projected[..., :wide]) * projected[..., wide:]).astype(jnp.bfloat16)
    hidden = hidden.reshape(local_count, expert_count * capacity, wide)
    row_shares = jnp.transpose(arrived_shares, (1, 0, 2)).reshape(local_count, -1)
    weighted = hidden.astype(jnp.float32) * row_shares[..., None]
    high = weighted.astype(jnp.bfloat16)
    low = (weighted - high.astype(jnp.float32)).astype(jnp.bfloat16)
    gram = jnp.einsum("lrf,lrg->lfg", hidden, high, preferred_element_type=jnp.float32)
    gram = gram + jnp.einsum("lrf,lrg->lfg", hidden, low, preferred_element_type=jnp.float32)
    gram = lax.psum_scatter(gram * norm_factor, "seq", scatter_dimension=1, tiled=True)
    full_max = lax.pmax(channel_max, "seq")
    part = width // seq_count
    maxima = lax.dynamic_slice_in_dim(full_max, lax.axis_index("seq") * part, part, 1)
    return (gram, maxima)


def body(tokens, routes, gate_shares, gate_up):
    expert_count = lax.axis_size("expert")
    local_count = gate_up.shape[0]
    rows = tokens.shape[0]
    capacity = 2 * rows * routes.shape[1] // (local_count * expert_count)
    whole_rows = rows <= local_count * capacity
    shaped = lax.axis_size("seq") == 2 and expert_count == 16 and local_count == 2
    plan = gather_body if whole_rows and shaped else routed_body
    return plan(capacity, tokens, routes, gate_shares, gate_up)


def solution(mesh):
    return jax.shard_map(
        body,
        mesh=mesh,
        in_specs=(
            P(("seq", "expert"), None),
            P(("seq", "expert"), None),
            P(("seq", "expert"), None),
            P("expert", "seq", None),
        ),
        out_specs=(P("expert", "seq", None), P("expert", "seq")),
        check_vma=False,
    )
```

```python
import functools
import math

import jax
import jax.numpy as jnp
from jax import lax
from jax.experimental import pallas as pl
from jax.experimental.pallas import tpu as pltpu
from jax.sharding import PartitionSpec as P

VMEM_LIMIT = 18 * 1024 * 1024
FIRST_LIMIT = 60 * 1024 * 1024
VM = pl.BlockSpec(memory_space=pltpu.VMEM)
SM = pl.BlockSpec(memory_space=pltpu.SMEM)


def params(limit=VMEM_LIMIT):
    return pltpu.CompilerParams(vmem_limit_bytes=limit)


def cost(flops, moved):
    return pl.CostEstimate(flops=16 * int(flops), bytes_accessed=16 * int(moved), transcendentals=0)


def pack_kernel(experts, tok_ref, routes_ref, shares_ref, w_ref, out_ref, piece_ref, small_ref, sems):
    rows, width = tok_ref.shape
    top = routes_ref.shape[0]
    extra = out_ref.shape[1] - width
    copies = [
        pltpu.make_async_copy(source, target, sems.at[k])
        for k, (source, target) in enumerate(
            (
                (routes_ref, small_ref.at[0]),
                (shares_ref, small_ref.at[1]),
                (tok_ref, out_ref.at[:, pl.ds(0, width)]),
                (w_ref.at[pl.ds(0, piece_ref.shape[0]), :], piece_ref),
            )
        )
    ]
    for copy in copies:
        copy.start()
    copies[0].wait()
    copies[1].wait()
    routes, shares = small_ref[0].T, small_ref[1].T
    lane = lax.broadcasted_iota(jnp.int32, (rows, extra), 1)
    expert = jnp.where(lane < experts, lane, lane - experts)
    value = jnp.zeros((rows, extra), jnp.int32)
    for k in range(top):
        value = value + jnp.where(routes[:, k : k + 1] == expert, shares[:, k : k + 1], 0)
    share = value.astype(jnp.float32) / 65536.0
    high = share.astype(jnp.bfloat16).astype(jnp.float32)
    low = share - high
    out_ref[:, width:] = jnp.where(lane < experts, high, low).astype(jnp.bfloat16)
    copies[2].wait()
    copies[3].wait()


def pick_kernel(experts, cap, count, apart, *refs):
    where_ref = refs[0]
    blocks = refs[1 : 1 + count]
    own_ref, *other_refs = refs[1 + count :]
    rows, full = blocks[0].shape
    local = own_ref.shape[0] // (count * cap)
    extra = -(-2 * experts // 128) * 128
    width = full - extra
    lane = lax.broadcasted_iota(jnp.int32, (1, extra), 1)
    slot = lax.broadcasted_iota(jnp.int32, (1, cap), 1).astype(jnp.float32)
    below = (
        lax.broadcasted_iota(jnp.int32, (rows, rows), 0)
        > lax.broadcasted_iota(jnp.int32, (rows, rows), 1)
    ).astype(jnp.bfloat16)
    firsts = (where_ref[0] * local, where_ref[1] * local)
    lives = []
    for block in blocks:
        side = block[:, width:].astype(jnp.float32)
        lives.append(jnp.where((side > 0.0) & (lane < experts), 1.0, 0.0))
    live = jnp.concatenate(lives, axis=1)
    rank = jnp.dot(below, live.astype(jnp.bfloat16), preferred_element_type=jnp.float32)
    place = jnp.where(live > 0.0, rank, -1.0)
    picks = []
    for b in range(count):
        at = place[:, b * extra : (b + 1) * extra]
        mine = [
            jnp.sum(jnp.where(lane == first + i, at, 0.0), axis=1, keepdims=True)
            for first in firsts
            for i in range(local)
        ]
        pick = jnp.concatenate([jnp.where(m == slot, 1.0, 0.0) for m in mine], axis=1)
        picks.append(pick.astype(jnp.bfloat16))
    for b, block in enumerate(blocks):
        taken = lax.dot_general(
            picks[b], block[...], (((0,), (0,)), ((), ())), preferred_element_type=jnp.float32
        ).astype(jnp.bfloat16)
        for i in range(local):
            at = (i * count + b) * cap
            own_ref[at : at + cap, :] = taken[i * cap : (i + 1) * cap]
            got = (local + i) * cap
            ref, at = (other_refs[i], b * cap) if apart else (other_refs[0], at)
            ref[at : at + cap, :] = taken[got : got + cap]


def picked(experts, cap, local, where, blocks, apart=False):
    count = len(blocks)
    rows, full = blocks[0].shape
    out = [jax.ShapeDtypeStruct((local * count * cap, full), jnp.bfloat16)]
    one = jax.ShapeDtypeStruct((count * cap, full), jnp.bfloat16)
    out += [one] * local if apart else out
    return pl.pallas_call(
        functools.partial(pick_kernel, experts, cap, count, apart),
        out_shape=tuple(out),
        in_specs=[SM] + [VM] * count,
        out_specs=(VM,) * len(out),
        compiler_params=params(),
        cost_estimate=cost(1, 1) if apart else cost(
            4 * count * rows * local * cap * full, 2 * count * full * (rows + 2 * local * cap)
        ),
        name="picked_rows",
    )(where, *blocks)


def hidden_terms(value, share):
    wide = value.shape[1] // 2
    gate = value[:, :wide]
    hidden = (gate / (1.0 + jnp.exp(-gate)) * value[:, wide:]).astype(jnp.bfloat16)
    weighted = hidden.astype(jnp.float32) * share
    high = weighted.astype(jnp.bfloat16)
    low = (weighted - high.astype(jnp.float32)).astype(jnp.bfloat16)
    return hidden, high, low


def gram_terms(hidden_ref, weighted_ref):
    wide = hidden_ref.shape[1]
    both = lax.dot_general(
        hidden_ref[...],
        weighted_ref[...],
        (((0,), (0,)), ((), ())),
        preferred_element_type=jnp.float32,
    )
    return both[:, :wide] + both[:, wide:]


def hidden_and_gram(value, share, hidden_ref, weighted_ref):
    wide = hidden_ref.shape[1]
    hidden_ref[...], weighted_ref[:, :wide], weighted_ref[:, wide:] = hidden_terms(value, share)
    return gram_terms(hidden_ref, weighted_ref)


def give_out(total, seq, own_ref, send_ref, hold_ref):
    hold_ref[...] = total
    part = own_ref.shape[0]
    own_ref[...] = hold_ref[pl.ds(pl.multiple_of(seq * part, 16), part), :]
    send_ref[...] = hold_ref[pl.ds(pl.multiple_of((1 - seq) * part, 16), part), :].astype(
        jnp.bfloat16
    )


def experts_kernel(experts, pieces, kinds, carried, final, factor, *refs):
    where_ref, w_ref = refs[:2]
    far_refs = refs[2 : 2 + pieces]
    rest = refs[2 + pieces :]
    groups = []
    for kind in kinds:
        groups.append(rest[:kind])
        rest = rest[kind:]
    if carried:
        gram_in_ref, max_in_ref = rest[:2]
        rest = rest[2:]
    max_ref, p_ref, late_ref = rest[:3]
    hidden_ref, weighted_ref = rest[-2:]
    rest = rest[3:-2]
    local, depth, fan = w_ref.shape
    extra = -(-2 * experts // 128) * 128
    width = groups[0][0].shape[1] - extra
    lane = lax.broadcasted_iota(jnp.int32, (1, extra), 1)
    first, seq = where_ref[0] * local, where_ref[2]
    near, far = pl.multiple_of(seq * depth, 128), pl.multiple_of((1 - seq) * depth, 128)

    def part(i, columns):
        pieces_of = []
        for g in groups:
            if len(g) == 1:
                n = g[0].shape[0] // local
                pieces_of.append(g[0][i * n : (i + 1) * n, columns])
            else:
                pieces_of.append(g[i][:, columns])
        return jnp.concatenate(pieces_of, axis=0)

    def share_of(i):
        both = (lane == first + i) | (lane == experts + first + i)
        side = part(i, slice(width, width + extra)).astype(jnp.float32)
        return jnp.sum(jnp.where(both, side, 0.0), axis=1, keepdims=True)

    def product(a, w):
        return jnp.dot(a, w, preferred_element_type=jnp.float32)

    values = [product(part(i, pl.ds(near, depth)), w_ref[i]) for i in range(local)]
    at = 0
    for far_ref in far_refs:
        end = at + far_ref.shape[0]
        for i in range(local):
            low, high = max(at, i * depth), min(end, (i + 1) * depth)
            if low < high:
                columns = pl.ds(pl.multiple_of(far + low - i * depth, 128), high - low)
                values[i] = values[i] + product(part(i, columns), far_ref[low - at : high - at, :])
        at = end
    known = at - depth
    total = hidden_and_gram(values[0], share_of(0), hidden_ref, weighted_ref)
    p_ref[:, :fan] = values[1]
    p_ref[:, fan:] = jnp.broadcast_to(share_of(1), (p_ref.shape[0], 128))
    late_ref[...] = part(1, pl.ds(pl.multiple_of(far + known, 128), depth - known))
    for i in range(local):
        size = jnp.abs(part(i, slice(0, width)))
        largest = max_in_ref[i * 16 : (i + 1) * 16, :] if carried else size[:16]
        for r in range(0 if carried else 16, size.shape[0], 16):
            largest = jnp.maximum(largest, size[r : r + 16])
        max_ref[i * 16 : (i + 1) * 16, :] = largest
    if carried:
        total = total + gram_in_ref[...]
    if final:
        give_out(total * factor, seq, *rest)
    else:
        rest[0][...] = total


def experts_of(experts, where, weights, far, groups, carried, final, factor):
    local, depth, fan = weights.shape
    wide = fan // 2
    kinds = tuple(len(g) for g in groups)
    groups = [array for g in groups for array in g]
    rows = sum(g.shape[0] for g in groups) // local
    width = 2 * depth
    out = [
        jax.ShapeDtypeStruct((local * 16, width), jnp.bfloat16),
        jax.ShapeDtypeStruct((rows, fan + 128), jnp.float32),
        jax.ShapeDtypeStruct((rows, 2 * depth - depth_of(far)), jnp.bfloat16),
    ]
    scratch = [pltpu.VMEM((rows, wide), jnp.bfloat16), pltpu.VMEM((rows, fan), jnp.bfloat16)]
    if final:
        out += [
            jax.ShapeDtypeStruct((wide // 2, wide), jnp.float32),
            jax.ShapeDtypeStruct((wide // 2, wide), jnp.bfloat16),
        ]
        scratch = [pltpu.VMEM((wide, wide), jnp.float32)] + scratch
    else:
        out.append(jax.ShapeDtypeStruct((wide, wide), jnp.float32))
    ins = [weights, *far, *groups, *(carried or ())]
    return pl.pallas_call(
        functools.partial(experts_kernel, experts, len(far), kinds, bool(carried), final, factor),
        out_shape=tuple(out),
        in_specs=[SM] + [VM] * len(ins),
        out_specs=(VM,) * len(out),
        scratch_shapes=scratch,
        compiler_params=params(),
        cost_estimate=cost(1, 1) if carried else cost(2 * rows * (depth + depth_of(far)) * fan, 0),
        name="expert_terms",
    )(where, *ins)


def last_kernel(step, firsts, factor, *refs):
    where_ref, w_ref = refs[:2]
    count = len(firsts) - 1
    groups = refs[2 : 2 + 2 * count]
    own_ref, send_ref, hold_ref, hidden_ref, weighted_ref = refs[2 + 2 * count :]
    fan = w_ref.shape[1]
    wide = fan // 2
    now = pl.program_id(0)
    for g in range(count):

        @pl.when((now >= firsts[g]) & (now < firsts[g + 1]))
        def _(g=g):
            x_ref, p_ref = groups[2 * g : 2 * g + 2]
            value = p_ref[:, :fan] + jnp.dot(
                x_ref[:, x_ref.shape[1] - w_ref.shape[0] :],
                w_ref[...],
                preferred_element_type=jnp.float32,
            )
            hidden, high, low = hidden_terms(value, p_ref[:, fan : fan + 1])
            rows = pl.ds(pl.multiple_of(now * step, step), step)
            hidden_ref[rows, :] = hidden
            weighted_ref[rows, :wide] = high
            weighted_ref[rows, wide:] = low

    @pl.when(now == firsts[-1] - 1)
    def _():
        total = gram_terms(hidden_ref, weighted_ref)
        give_out(total * factor, where_ref[2], own_ref, send_ref, hold_ref)


def last_of(where, weights, parts, factor):
    depth, fan = weights.shape
    wide = fan // 2
    rows = [p.shape[0] for _, p in parts]
    step = functools.reduce(math.gcd, rows, 256)
    firsts = [0]
    ins, specs = [], []
    for x, p in parts:
        first, number = firsts[-1], p.shape[0] // step
        firsts.append(first + number)
        for array in (x, p):
            ins.append(array)
            specs.append(
                pl.BlockSpec(
                    (step, array.shape[1]),
                    lambda g, first=first, number=number: (jnp.clip(g - first, 0, number - 1), 0),
                )
            )
    return pl.pallas_call(
        functools.partial(last_kernel, step, tuple(firsts), factor),
        grid=(firsts[-1],),
        out_shape=(
            jax.ShapeDtypeStruct((wide // 2, wide), jnp.float32),
            jax.ShapeDtypeStruct((wide // 2, wide), jnp.bfloat16),
        ),
        in_specs=[SM, pl.BlockSpec(weights.shape, lambda g: (0, 0))] + specs,
        out_specs=(pl.BlockSpec((wide // 2, wide), lambda g: (0, 0)),) * 2,
        scratch_shapes=[
            pltpu.VMEM((wide, wide), jnp.float32),
            pltpu.VMEM((sum(rows), wide), jnp.bfloat16),
            pltpu.VMEM((sum(rows), fan), jnp.bfloat16),
        ],
        compiler_params=params(),
        cost_estimate=cost(2 * sum(rows) * depth * fan, 0),
        name="last_terms",
    )(where, weights, *ins)


def depth_of(weights):
    return sum(w.shape[0] for w in weights)


def split_kernel(pieces, w_ref, after_ref, *refs):
    outs, sems = refs[: len(pieces)], refs[len(pieces)]
    copies = [
        pltpu.make_async_copy(w_ref.at[pl.ds(r, n), :], out, sems.at[k])
        for k, ((r, n), out) in enumerate(zip(pieces, outs))
    ]
    for copy in copies:
        copy.start()
    for copy in copies:
        copy.wait()


def split_of(flat, after, pieces):
    anywhere = pl.BlockSpec(memory_space=pl.ANY)
    return pl.pallas_call(
        functools.partial(split_kernel, pieces),
        out_shape=tuple(jax.ShapeDtypeStruct((n, flat.shape[1]), flat.dtype) for _, n in pieces),
        in_specs=[anywhere, anywhere],
        out_specs=(anywhere,) * len(pieces),
        scratch_shapes=[pltpu.SemaphoreType.DMA((len(pieces),))],
        compiler_params=params(),
        cost_estimate=cost(0, 0),
        name="weight_pieces",
    )(flat, after)


def tie(*arrays):
    return lax.optimization_barrier(arrays)


def gather_body(capacity, tokens, routes, gate_shares, gate_up):
    tok_rows, width = tokens.shape
    top_count = routes.shape[1]
    expert_count = lax.axis_size("expert")
    seq_count = lax.axis_size("seq")
    local_count, depth, fan = gate_up.shape
    all_experts = local_count * expert_count
    factor = all_experts / (tok_rows * seq_count * expert_count * top_count)
    columns = expert_count // 4

    def moved(array, target):
        places = [(z, x, c) for z in range(columns) for x in range(2) for c in range(2)]
        number = {place: n for n, place in enumerate(places)}
        return lax.ppermute(array, "expert", [(number[p], number[target(*p)]) for p in places])

    def hop(array, pairs):
        return lax.ppermute(
            array, "expert", [(4 * a + n, 4 * b + n) for a, b in pairs for n in range(4)]
        )

    def along_x(array):
        return moved(array, lambda z, x, c: (z, 1 - x, c))

    def along_core(array):
        return moved(array, lambda z, x, c: (z, x, 1 - c))

    def swapped(array):
        return lax.ppermute(array, "seq", [(0, 1), (1, 0)])

    index, seq = lax.axis_index("expert"), lax.axis_index("seq")
    where = jnp.stack([index, index + 1 - 2 * (index % 2), seq]).astype(jnp.int32)
    extra = -(-2 * all_experts // 128) * 128
    flat = gate_up.reshape(local_count * depth, fan)
    cuts = [depth // 8 * n for n in (0, 7, 9, 16)]
    spans = [(low, high - low) for low, high in zip(cuts, cuts[1:])]
    anywhere = pl.BlockSpec(memory_space=pl.ANY)
    own, piece = pl.pallas_call(
        functools.partial(pack_kernel, all_experts),
        out_shape=(
            jax.ShapeDtypeStruct((tok_rows, width + extra), jnp.bfloat16),
            jax.ShapeDtypeStruct((spans[0][1], fan), jnp.bfloat16),
        ),
        in_specs=[anywhere] * 4,
        out_specs=(VM, VM),
        scratch_shapes=[
            pltpu.VMEM((2, top_count, tok_rows), jnp.int32),
            pltpu.SemaphoreType.DMA((4,)),
        ],
        compiler_params=params(FIRST_LIMIT),
        cost_estimate=cost(0, 4 * tok_rows * width),
        name="packed_tokens",
    )(tokens, routes.T, gate_shares.T, flat)
    far1 = swapped(piece)
    pick = functools.partial(picked, all_experts, capacity, local_count, where)
    terms = functools.partial(experts_of, all_experts, where, gate_up)

    outer = (index // 4 == 0) | (index // 4 == columns - 1)
    za, zm, x0 = hop(own, ((0, 1), (1, 0), (2, 3), (3, 2))), hop(own, ((1, 2), (2, 1))), along_x(own)
    pieces = split_of(flat, own, tuple(spans[1:]))
    own, za, zm, x0, *pieces = tie(own, za, zm, x0, *pieces)
    zo, zi, xa = hop(zm, ((1, 0), (2, 3))), hop(za, ((1, 2), (2, 1))), along_x(za)
    m0, o0 = pick((own, x0))
    zc = jnp.where(outer, zo, zi)
    zc, xa, o0, far1, zm, za, *pieces = tie(zc, xa, o0, far1, zm, za, *pieces)
    zr, xc = hop(zc, ((1, 0), (2, 3))), along_x(zc)
    far2 = swapped(pieces[0])
    r0 = along_core(o0)
    m1, o1 = pick((za, xa))
    zb = jnp.where(outer, zr, zm)
    zb, xc, r0, o1, zc, far2, *pieces = tie(zb, xc, r0, o1, zc, far2, *pieces)
    xb = along_x(zb)
    r1 = along_core(o1)
    far3 = swapped(pieces[1])
    m2, o2 = pick((zc, xc))
    max0, p0, late0, gram0 = terms((far1, far2), ((m0,), (r0,), (m1,), (r1,)), None, False, factor)
    xb, o2, gram0, max0, zb = tie(xb, o2, gram0, max0, zb)
    r2 = along_core(o2)
    m3, *o3 = pick((zb, xb), apart=True)
    r3 = tuple(along_core(o) for o in o3)
    max0, p1, late1, gram0 = terms((far1, far2), ((m2,), (r2,)), (gram0, max0), False, factor)
    largest, p2, late2, own0, send0 = terms(
        (far1, far2), ((m3,), r3), (gram0, max0), True, factor
    )
    got0 = swapped(send0)
    largest = jnp.max(largest.reshape(local_count, -1, width), axis=1).astype(jnp.float32)
    keep = lax.dynamic_slice_in_dim(largest, seq * depth, depth, 1)
    give = lax.dynamic_slice_in_dim(largest, (1 - seq) * depth, depth, 1)
    maxima = jnp.maximum(keep, swapped(give))
    own1, send1 = last_of(where, far3, ((late0, p0), (late1, p1), (late2, p2)), factor)
    whole0, send1 = tie(own0 + got0.astype(jnp.float32), send1)
    got1 = swapped(send1)
    gram = jnp.stack([whole0, own1 + got1.astype(jnp.float32)])
    return (gram, maxima)


def routed_body(capacity, tokens, routes, gate_shares, gate_up):
    tok_rows, width = tokens.shape
    top_count = routes.shape[1]
    expert_count = lax.axis_size("expert")
    seq_count = lax.axis_size("seq")
    local_count, _, fan = gate_up.shape
    wide = fan // 2
    all_experts = local_count * expert_count
    norm_factor = all_experts / (tok_rows * seq_count * expert_count * top_count)
    chosen = routes.reshape(-1)
    shares = gate_shares.reshape(-1).astype(jnp.float32) / 65536.0
    one_hot = (chosen[:, None] == jnp.arange(all_experts, dtype=jnp.int32)[None, :]).astype(jnp.int32)
    ranked = jnp.sum((jnp.cumsum(one_hot, axis=0) - one_hot) * one_hot, axis=1)
    slot_index = chosen * capacity + ranked
    token_index = jnp.arange(tok_rows * top_count, dtype=jnp.int32) // top_count
    outgoing = (
        jnp.zeros((all_experts * capacity, width), jnp.bfloat16)
        .at[slot_index]
        .set(tokens[token_index])
        .reshape(expert_count, local_count, capacity, width)
    )
    out_shares = (
        jnp.zeros((all_experts * capacity,), jnp.float32)
        .at[slot_index]
        .set(shares)
        .reshape(expert_count, local_count, capacity)
    )
    arrived = lax.all_to_all(outgoing, "expert", split_axis=0, concat_axis=0, tiled=True)
    arrived_shares = lax.all_to_all(out_shares, "expert", split_axis=0, concat_axis=0, tiled=True)
    channel_max = jnp.max(
        jnp.where(arrived_shares[..., None] > 0.0, jnp.abs(arrived), 0), axis=(0, 2)
    ).astype(jnp.float32)
    projected = jnp.einsum(
        "slcd,ldf->lscf",
        arrived,
        lax.all_gather(gate_up, "seq", axis=1, tiled=True),
        preferred_element_type=jnp.float32,
    )
    hidden = (jax.nn.silu(projected[..., :wide]) * projected[..., wide:]).astype(jnp.bfloat16)
    hidden = hidden.reshape(local_count, expert_count * capacity, wide)
    row_shares = jnp.transpose(arrived_shares, (1, 0, 2)).reshape(local_count, -1)
    weighted = hidden.astype(jnp.float32) * row_shares[..., None]
    high = weighted.astype(jnp.bfloat16)
    low = (weighted - high.astype(jnp.float32)).astype(jnp.bfloat16)
    gram = jnp.einsum("lrf,lrg->lfg", hidden, high, preferred_element_type=jnp.float32)
    gram = gram + jnp.einsum("lrf,lrg->lfg", hidden, low, preferred_element_type=jnp.float32)
    gram = lax.psum_scatter(gram * norm_factor, "seq", scatter_dimension=1, tiled=True)
    full_max = lax.pmax(channel_max, "seq")
    part = width // seq_count
    maxima = lax.dynamic_slice_in_dim(full_max, lax.axis_index("seq") * part, part, 1)
    return (gram, maxima)


def body(tokens, routes, gate_shares, gate_up):
    expert_count = lax.axis_size("expert")
    local_count = gate_up.shape[0]
    rows = tokens.shape[0]
    capacity = 2 * rows * routes.shape[1] // (local_count * expert_count)
    whole_rows = rows <= local_count * capacity
    shaped = lax.axis_size("seq") == 2 and expert_count == 16 and local_count == 2
    plan = gather_body if whole_rows and shaped else routed_body
    return plan(capacity, tokens, routes, gate_shares, gate_up)


def solution(mesh):
    return jax.shard_map(
        body,
        mesh=mesh,
        in_specs=(
            P(("seq", "expert"), None),
            P(("seq", "expert"), None),
            P(("seq", "expert"), None),
            P("expert", "seq", None),
        ),
        out_specs=(P("expert", "seq", None), P("expert", "seq")),
        check_vma=False,
    )
```

```python
import functools
import math

import jax
import jax.numpy as jnp
from jax import lax
from jax.experimental import pallas as pl
from jax.experimental.pallas import tpu as pltpu
from jax.sharding import PartitionSpec as P

VMEM_LIMIT = 18 * 1024 * 1024
FIRST_LIMIT = 60 * 1024 * 1024
VM = pl.BlockSpec(memory_space=pltpu.VMEM)
SM = pl.BlockSpec(memory_space=pltpu.SMEM)


def params(limit=VMEM_LIMIT):
    return pltpu.CompilerParams(vmem_limit_bytes=limit)


def cost(flops, moved):
    return pl.CostEstimate(flops=16 * int(flops), bytes_accessed=16 * int(moved), transcendentals=0)


def pack_kernel(experts, tok_ref, routes_ref, shares_ref, w_ref, out_ref, piece_ref, small_ref, sems):
    rows, width = tok_ref.shape
    top = routes_ref.shape[0]
    extra = out_ref.shape[1] - width
    copies = [
        pltpu.make_async_copy(source, target, sems.at[k])
        for k, (source, target) in enumerate(
            (
                (routes_ref, small_ref.at[0]),
                (shares_ref, small_ref.at[1]),
                (tok_ref, out_ref.at[:, pl.ds(0, width)]),
                (w_ref.at[pl.ds(0, piece_ref.shape[0]), :], piece_ref),
            )
        )
    ]
    for copy in copies:
        copy.start()
    copies[0].wait()
    copies[1].wait()
    routes, shares = small_ref[0].T, small_ref[1].T
    lane = lax.broadcasted_iota(jnp.int32, (rows, extra), 1)
    expert = jnp.where(lane < experts, lane, lane - experts)
    value = jnp.zeros((rows, extra), jnp.int32)
    for k in range(top):
        value = value + jnp.where(routes[:, k : k + 1] == expert, shares[:, k : k + 1], 0)
    share = value.astype(jnp.float32) / 65536.0
    high = share.astype(jnp.bfloat16).astype(jnp.float32)
    low = share - high
    out_ref[:, width:] = jnp.where(lane < experts, high, low).astype(jnp.bfloat16)
    copies[2].wait()
    copies[3].wait()


def pick_kernel(experts, cap, count, apart, *refs):
    where_ref = refs[0]
    blocks = refs[1 : 1 + count]
    own_ref, *other_refs = refs[1 + count :]
    rows, full = blocks[0].shape
    local = own_ref.shape[0] // (count * cap)
    extra = -(-2 * experts // 128) * 128
    width = full - extra
    lane = lax.broadcasted_iota(jnp.int32, (1, extra), 1)
    slot = lax.broadcasted_iota(jnp.int32, (1, cap), 1).astype(jnp.float32)
    below = (
        lax.broadcasted_iota(jnp.int32, (rows, rows), 0)
        > lax.broadcasted_iota(jnp.int32, (rows, rows), 1)
    ).astype(jnp.bfloat16)
    firsts = (where_ref[0] * local, where_ref[1] * local)
    lives = []
    for block in blocks:
        side = block[:, width:].astype(jnp.float32)
        lives.append(jnp.where((side > 0.0) & (lane < experts), 1.0, 0.0))
    live = jnp.concatenate(lives, axis=1)
    rank = jnp.dot(below, live.astype(jnp.bfloat16), preferred_element_type=jnp.float32)
    place = jnp.where(live > 0.0, rank, -1.0)
    picks = []
    for b in range(count):
        at = place[:, b * extra : (b + 1) * extra]
        mine = [
            jnp.sum(jnp.where(lane == first + i, at, 0.0), axis=1, keepdims=True)
            for first in firsts
            for i in range(local)
        ]
        pick = jnp.concatenate([jnp.where(m == slot, 1.0, 0.0) for m in mine], axis=1)
        picks.append(pick.astype(jnp.bfloat16))
    for b, block in enumerate(blocks):
        taken = lax.dot_general(
            picks[b], block[...], (((0,), (0,)), ((), ())), preferred_element_type=jnp.float32
        ).astype(jnp.bfloat16)
        for i in range(local):
            at = (i * count + b) * cap
            own_ref[at : at + cap, :] = taken[i * cap : (i + 1) * cap]
            got = (local + i) * cap
            ref, at = (other_refs[i], b * cap) if apart else (other_refs[0], at)
            ref[at : at + cap, :] = taken[got : got + cap]


def picked(experts, cap, local, where, blocks, apart=False):
    count = len(blocks)
    rows, full = blocks[0].shape
    out = [jax.ShapeDtypeStruct((local * count * cap, full), jnp.bfloat16)]
    one = jax.ShapeDtypeStruct((count * cap, full), jnp.bfloat16)
    out += [one] * local if apart else out
    return pl.pallas_call(
        functools.partial(pick_kernel, experts, cap, count, apart),
        out_shape=tuple(out),
        in_specs=[SM] + [VM] * count,
        out_specs=(VM,) * len(out),
        compiler_params=params(),
        cost_estimate=cost(1, 1) if apart else cost(
            4 * count * rows * local * cap * full, 2 * count * full * (rows + 2 * local * cap)
        ),
        name="picked_rows",
    )(where, *blocks)


def hidden_terms(value, share):
    wide = value.shape[1] // 2
    gate = value[:, :wide]
    hidden = (gate / (1.0 + jnp.exp(-gate)) * value[:, wide:]).astype(jnp.bfloat16)
    weighted = hidden.astype(jnp.float32) * share
    high = weighted.astype(jnp.bfloat16)
    low = (weighted - high.astype(jnp.float32)).astype(jnp.bfloat16)
    return hidden, high, low


def gram_terms(hidden_ref, weighted_ref):
    wide = hidden_ref.shape[1]
    both = lax.dot_general(
        hidden_ref[...],
        weighted_ref[...],
        (((0,), (0,)), ((), ())),
        preferred_element_type=jnp.float32,
    )
    return both[:, :wide] + both[:, wide:]


def hidden_and_gram(value, share, hidden_ref, weighted_ref):
    wide = hidden_ref.shape[1]
    hidden_ref[...], weighted_ref[:, :wide], weighted_ref[:, wide:] = hidden_terms(value, share)
    return gram_terms(hidden_ref, weighted_ref)


def give_out(total, seq, own_ref, send_ref, hold_ref):
    hold_ref[...] = total
    part = own_ref.shape[0]
    own_ref[...] = hold_ref[pl.ds(pl.multiple_of(seq * part, 16), part), :]
    send_ref[:part, :] = hold_ref[pl.ds(pl.multiple_of((1 - seq) * part, 16), part), :].astype(
        jnp.bfloat16
    )


def experts_kernel(experts, pieces, kinds, carried, final, factor, *refs):
    where_ref, w_ref = refs[:2]
    far_refs = refs[2 : 2 + pieces]
    rest = refs[2 + pieces :]
    groups = []
    for kind in kinds:
        groups.append(rest[:kind])
        rest = rest[kind:]
    if carried:
        gram_in_ref, max_in_ref = rest[:2]
        rest = rest[2:]
    max_ref, p_ref, late_ref = rest[:3]
    hidden_ref, weighted_ref = rest[-2:]
    rest = rest[3:-2]
    local, depth, fan = w_ref.shape
    extra = -(-2 * experts // 128) * 128
    width = groups[0][0].shape[1] - extra
    lane = lax.broadcasted_iota(jnp.int32, (1, extra), 1)
    first, seq = where_ref[0] * local, where_ref[2]
    near, far = pl.multiple_of(seq * depth, 128), pl.multiple_of((1 - seq) * depth, 128)

    def part(i, columns):
        pieces_of = []
        for g in groups:
            if len(g) == 1:
                n = g[0].shape[0] // local
                pieces_of.append(g[0][i * n : (i + 1) * n, columns])
            else:
                pieces_of.append(g[i][:, columns])
        return jnp.concatenate(pieces_of, axis=0)

    def share_of(i):
        both = (lane == first + i) | (lane == experts + first + i)
        side = part(i, slice(width, width + extra)).astype(jnp.float32)
        return jnp.sum(jnp.where(both, side, 0.0), axis=1, keepdims=True)

    def product(a, w):
        return jnp.dot(a, w, preferred_element_type=jnp.float32)

    values = [product(part(i, pl.ds(near, depth)), w_ref[i]) for i in range(local)]
    at = 0
    for far_ref in far_refs:
        end = at + far_ref.shape[0]
        for i in range(local):
            low, high = max(at, i * depth), min(end, (i + 1) * depth)
            if low < high:
                columns = pl.ds(pl.multiple_of(far + low - i * depth, 128), high - low)
                values[i] = values[i] + product(part(i, columns), far_ref[low - at : high - at, :])
        at = end
    known = at - depth
    total = hidden_and_gram(values[0], share_of(0), hidden_ref, weighted_ref)
    p_ref[:, :fan] = values[1]
    p_ref[:, fan:] = jnp.broadcast_to(share_of(1), (p_ref.shape[0], 128))
    late_ref[...] = part(1, pl.ds(pl.multiple_of(far + known, 128), depth - known))
    for i in range(local):
        size = jnp.abs(part(i, slice(0, width)))
        largest = max_in_ref[i * 16 : (i + 1) * 16, :] if carried else size[:16]
        for r in range(0 if carried else 16, size.shape[0], 16):
            largest = jnp.maximum(largest, size[r : r + 16])
        max_ref[i * 16 : (i + 1) * 16, :] = largest
    if carried:
        total = total + gram_in_ref[...]
    if final:
        give_out(total * factor, seq, *rest)
        part = rest[0].shape[0]
        rows = []
        for i in range(local):
            found = max_ref[i * 16 : (i + 1) * 16, pl.ds(far, depth)].astype(jnp.float32)
            found = jnp.max(found, axis=0, keepdims=True)
            rows += [found[:, c : c + 128] for c in range(0, depth, 128)]
        rest[1][part:, :] = jnp.zeros((len(rows), rest[1].shape[1]), jnp.bfloat16)
        rest[1][part:, :128] = jnp.concatenate(rows, axis=0).astype(jnp.bfloat16)
    else:
        rest[0][...] = total


def experts_of(experts, where, weights, far, groups, carried, final, factor):
    local, depth, fan = weights.shape
    wide = fan // 2
    kinds = tuple(len(g) for g in groups)
    groups = [array for g in groups for array in g]
    rows = sum(g.shape[0] for g in groups) // local
    width = 2 * depth
    out = [
        jax.ShapeDtypeStruct((local * 16, width), jnp.bfloat16),
        jax.ShapeDtypeStruct((rows, fan + 128), jnp.float32),
        jax.ShapeDtypeStruct((rows, 2 * depth - depth_of(far)), jnp.bfloat16),
    ]
    scratch = [pltpu.VMEM((rows, wide), jnp.bfloat16), pltpu.VMEM((rows, fan), jnp.bfloat16)]
    if final:
        out += [
            jax.ShapeDtypeStruct((wide // 2, wide), jnp.float32),
            jax.ShapeDtypeStruct((wide // 2 + local * depth // 128, wide), jnp.bfloat16),
        ]
        scratch = [pltpu.VMEM((wide, wide), jnp.float32)] + scratch
    else:
        out.append(jax.ShapeDtypeStruct((wide, wide), jnp.float32))
    ins = [weights, *far, *groups, *(carried or ())]
    return pl.pallas_call(
        functools.partial(experts_kernel, experts, len(far), kinds, bool(carried), final, factor),
        out_shape=tuple(out),
        in_specs=[SM] + [VM] * len(ins),
        out_specs=(VM,) * len(out),
        scratch_shapes=scratch,
        compiler_params=params(),
        cost_estimate=cost(1, 1) if carried else cost(2 * rows * (depth + depth_of(far)) * fan, 0),
        name="expert_terms",
    )(where, *ins)


def last_kernel(step, firsts, factor, *refs):
    where_ref, w_ref = refs[:2]
    count = len(firsts) - 1
    groups = refs[2 : 2 + 2 * count]
    own_ref, send_ref, hold_ref, hidden_ref, weighted_ref = refs[2 + 2 * count :]
    fan = w_ref.shape[1]
    wide = fan // 2
    now = pl.program_id(0)
    for g in range(count):

        @pl.when((now >= firsts[g]) & (now < firsts[g + 1]))
        def _(g=g):
            x_ref, p_ref = groups[2 * g : 2 * g + 2]
            value = p_ref[:, :fan] + jnp.dot(
                x_ref[:, x_ref.shape[1] - w_ref.shape[0] :],
                w_ref[...],
                preferred_element_type=jnp.float32,
            )
            hidden, high, low = hidden_terms(value, p_ref[:, fan : fan + 1])
            rows = pl.ds(pl.multiple_of(now * step, step), step)
            hidden_ref[rows, :] = hidden
            weighted_ref[rows, :wide] = high
            weighted_ref[rows, wide:] = low

    @pl.when(now == firsts[-1] - 1)
    def _():
        total = gram_terms(hidden_ref, weighted_ref)
        give_out(total * factor, where_ref[2], own_ref, send_ref, hold_ref)


def last_of(where, weights, parts, factor):
    depth, fan = weights.shape
    wide = fan // 2
    rows = [p.shape[0] for _, p in parts]
    step = functools.reduce(math.gcd, rows, 256)
    firsts = [0]
    ins, specs = [], []
    for x, p in parts:
        first, number = firsts[-1], p.shape[0] // step
        firsts.append(first + number)
        for array in (x, p):
            ins.append(array)
            specs.append(
                pl.BlockSpec(
                    (step, array.shape[1]),
                    lambda g, first=first, number=number: (jnp.clip(g - first, 0, number - 1), 0),
                )
            )
    return pl.pallas_call(
        functools.partial(last_kernel, step, tuple(firsts), factor),
        grid=(firsts[-1],),
        out_shape=(
            jax.ShapeDtypeStruct((wide // 2, wide), jnp.float32),
            jax.ShapeDtypeStruct((wide // 2, wide), jnp.bfloat16),
        ),
        in_specs=[SM, pl.BlockSpec(weights.shape, lambda g: (0, 0))] + specs,
        out_specs=(pl.BlockSpec((wide // 2, wide), lambda g: (0, 0)),) * 2,
        scratch_shapes=[
            pltpu.VMEM((wide, wide), jnp.float32),
            pltpu.VMEM((sum(rows), wide), jnp.bfloat16),
            pltpu.VMEM((sum(rows), fan), jnp.bfloat16),
        ],
        compiler_params=params(),
        cost_estimate=cost(2 * sum(rows) * depth * fan, 0),
        name="last_terms",
    )(where, weights, *ins)


def depth_of(weights):
    return sum(w.shape[0] for w in weights)


def split_kernel(pieces, w_ref, after_ref, *refs):
    outs, sems = refs[: len(pieces)], refs[len(pieces)]
    copies = [
        pltpu.make_async_copy(w_ref.at[pl.ds(r, n), :], out, sems.at[k])
        for k, ((r, n), out) in enumerate(zip(pieces, outs))
    ]
    for copy in copies:
        copy.start()
    for copy in copies:
        copy.wait()


def split_of(flat, after, pieces):
    anywhere = pl.BlockSpec(memory_space=pl.ANY)
    return pl.pallas_call(
        functools.partial(split_kernel, pieces),
        out_shape=tuple(jax.ShapeDtypeStruct((n, flat.shape[1]), flat.dtype) for _, n in pieces),
        in_specs=[anywhere, anywhere],
        out_specs=(anywhere,) * len(pieces),
        scratch_shapes=[pltpu.SemaphoreType.DMA((len(pieces),))],
        compiler_params=params(),
        cost_estimate=cost(0, 0),
        name="weight_pieces",
    )(flat, after)


def tie(*arrays):
    return lax.optimization_barrier(arrays)


def gather_body(capacity, tokens, routes, gate_shares, gate_up):
    tok_rows, width = tokens.shape
    top_count = routes.shape[1]
    expert_count = lax.axis_size("expert")
    seq_count = lax.axis_size("seq")
    local_count, depth, fan = gate_up.shape
    all_experts = local_count * expert_count
    factor = all_experts / (tok_rows * seq_count * expert_count * top_count)
    columns = expert_count // 4

    def moved(array, target):
        places = [(z, x, c) for z in range(columns) for x in range(2) for c in range(2)]
        number = {place: n for n, place in enumerate(places)}
        return lax.ppermute(array, "expert", [(number[p], number[target(*p)]) for p in places])

    def hop(array, pairs):
        return lax.ppermute(
            array, "expert", [(4 * a + n, 4 * b + n) for a, b in pairs for n in range(4)]
        )

    def along_x(array):
        return moved(array, lambda z, x, c: (z, 1 - x, c))

    def along_core(array):
        return moved(array, lambda z, x, c: (z, x, 1 - c))

    def swapped(array):
        return lax.ppermute(array, "seq", [(0, 1), (1, 0)])

    index, seq = lax.axis_index("expert"), lax.axis_index("seq")
    where = jnp.stack([index, index + 1 - 2 * (index % 2), seq]).astype(jnp.int32)
    extra = -(-2 * all_experts // 128) * 128
    flat = gate_up.reshape(local_count * depth, fan)
    cuts = [depth // 8 * n for n in (0, 7, 9, 16)]
    spans = [(low, high - low) for low, high in zip(cuts, cuts[1:])]
    anywhere = pl.BlockSpec(memory_space=pl.ANY)
    own, piece = pl.pallas_call(
        functools.partial(pack_kernel, all_experts),
        out_shape=(
            jax.ShapeDtypeStruct((tok_rows, width + extra), jnp.bfloat16),
            jax.ShapeDtypeStruct((spans[0][1], fan), jnp.bfloat16),
        ),
        in_specs=[anywhere] * 4,
        out_specs=(VM, VM),
        scratch_shapes=[
            pltpu.VMEM((2, top_count, tok_rows), jnp.int32),
            pltpu.SemaphoreType.DMA((4,)),
        ],
        compiler_params=params(FIRST_LIMIT),
        cost_estimate=cost(0, 4 * tok_rows * width),
        name="packed_tokens",
    )(tokens, routes.T, gate_shares.T, flat)
    far1 = swapped(piece)
    pick = functools.partial(picked, all_experts, capacity, local_count, where)
    terms = functools.partial(experts_of, all_experts, where, gate_up)

    outer = (index // 4 == 0) | (index // 4 == columns - 1)
    za, zm, x0 = hop(own, ((0, 1), (1, 0), (2, 3), (3, 2))), hop(own, ((1, 2), (2, 1))), along_x(own)
    pieces = split_of(flat, own, tuple(spans[1:]))
    own, za, zm, x0, *pieces = tie(own, za, zm, x0, *pieces)
    zo, zi, xa = hop(zm, ((1, 0), (2, 3))), hop(za, ((1, 2), (2, 1))), along_x(za)
    m0, o0 = pick((own, x0))
    zc = jnp.where(outer, zo, zi)
    zc, xa, o0, far1, zm, za, *pieces = tie(zc, xa, o0, far1, zm, za, *pieces)
    zr, xc = hop(zc, ((1, 0), (2, 3))), along_x(zc)
    far2 = swapped(pieces[0])
    r0 = along_core(o0)
    m1, o1 = pick((za, xa))
    zb = jnp.where(outer, zr, zm)
    zb, xc, r0, o1, zc, far2, *pieces = tie(zb, xc, r0, o1, zc, far2, *pieces)
    xb = along_x(zb)
    r1 = along_core(o1)
    far3 = swapped(pieces[1])
    m2, o2 = pick((zc, xc))
    max0, p0, late0, gram0 = terms((far1, far2), ((m0,), (r0,), (m1,), (r1,)), None, False, factor)
    xb, o2, gram0, max0, zb = tie(xb, o2, gram0, max0, zb)
    r2 = along_core(o2)
    m3, *o3 = pick((zb, xb), apart=True)
    r3 = tuple(along_core(o) for o in o3)
    max0, p1, late1, gram0 = terms((far1, far2), ((m2,), (r2,)), (gram0, max0), False, factor)
    largest, p2, late2, own0, send0 = terms(
        (far1, far2), ((m3,), r3), (gram0, max0), True, factor
    )
    got0 = swapped(send0)
    largest = jnp.max(largest.reshape(local_count, -1, width), axis=1).astype(jnp.float32)
    keep = lax.dynamic_slice_in_dim(largest, seq * depth, depth, 1)
    part = own0.shape[0]
    maxima = jnp.maximum(
        keep, got0[part:, :128].reshape(local_count, depth).astype(jnp.float32)
    )
    own1, send1 = last_of(where, far3, ((late0, p0), (late1, p1), (late2, p2)), factor)
    whole0, send1 = tie(own0 + got0[:part].astype(jnp.float32), send1)
    got1 = swapped(send1)
    gram = jnp.stack([whole0, own1 + got1.astype(jnp.float32)])
    return (gram, maxima)


def routed_body(capacity, tokens, routes, gate_shares, gate_up):
    tok_rows, width = tokens.shape
    top_count = routes.shape[1]
    expert_count = lax.axis_size("expert")
    seq_count = lax.axis_size("seq")
    local_count, _, fan = gate_up.shape
    wide = fan // 2
    all_experts = local_count * expert_count
    norm_factor = all_experts / (tok_rows * seq_count * expert_count * top_count)
    chosen = routes.reshape(-1)
    shares = gate_shares.reshape(-1).astype(jnp.float32) / 65536.0
    one_hot = (chosen[:, None] == jnp.arange(all_experts, dtype=jnp.int32)[None, :]).astype(jnp.int32)
    ranked = jnp.sum((jnp.cumsum(one_hot, axis=0) - one_hot) * one_hot, axis=1)
    slot_index = chosen * capacity + ranked
    token_index = jnp.arange(tok_rows * top_count, dtype=jnp.int32) // top_count
    outgoing = (
        jnp.zeros((all_experts * capacity, width), jnp.bfloat16)
        .at[slot_index]
        .set(tokens[token_index])
        .reshape(expert_count, local_count, capacity, width)
    )
    out_shares = (
        jnp.zeros((all_experts * capacity,), jnp.float32)
        .at[slot_index]
        .set(shares)
        .reshape(expert_count, local_count, capacity)
    )
    arrived = lax.all_to_all(outgoing, "expert", split_axis=0, concat_axis=0, tiled=True)
    arrived_shares = lax.all_to_all(out_shares, "expert", split_axis=0, concat_axis=0, tiled=True)
    channel_max = jnp.max(
        jnp.where(arrived_shares[..., None] > 0.0, jnp.abs(arrived), 0), axis=(0, 2)
    ).astype(jnp.float32)
    projected = jnp.einsum(
        "slcd,ldf->lscf",
        arrived,
        lax.all_gather(gate_up, "seq", axis=1, tiled=True),
        preferred_element_type=jnp.float32,
    )
    hidden = (jax.nn.silu(projected[..., :wide]) * projected[..., wide:]).astype(jnp.bfloat16)
    hidden = hidden.reshape(local_count, expert_count * capacity, wide)
    row_shares = jnp.transpose(arrived_shares, (1, 0, 2)).reshape(local_count, -1)
    weighted = hidden.astype(jnp.float32) * row_shares[..., None]
    high = weighted.astype(jnp.bfloat16)
    low = (weighted - high.astype(jnp.float32)).astype(jnp.bfloat16)
    gram = jnp.einsum("lrf,lrg->lfg", hidden, high, preferred_element_type=jnp.float32)
    gram = gram + jnp.einsum("lrf,lrg->lfg", hidden, low, preferred_element_type=jnp.float32)
    gram = lax.psum_scatter(gram * norm_factor, "seq", scatter_dimension=1, tiled=True)
    full_max = lax.pmax(channel_max, "seq")
    part = width // seq_count
    maxima = lax.dynamic_slice_in_dim(full_max, lax.axis_index("seq") * part, part, 1)
    return (gram, maxima)


def body(tokens, routes, gate_shares, gate_up):
    expert_count = lax.axis_size("expert")
    local_count = gate_up.shape[0]
    rows = tokens.shape[0]
    capacity = 2 * rows * routes.shape[1] // (local_count * expert_count)
    whole_rows = rows <= local_count * capacity
    shaped = lax.axis_size("seq") == 2 and expert_count == 16 and local_count == 2
    plan = gather_body if whole_rows and shaped else routed_body
    return plan(capacity, tokens, routes, gate_shares, gate_up)


def solution(mesh):
    return jax.shard_map(
        body,
        mesh=mesh,
        in_specs=(
            P(("seq", "expert"), None),
            P(("seq", "expert"), None),
            P(("seq", "expert"), None),
            P("expert", "seq", None),
        ),
        out_specs=(P("expert", "seq", None), P("expert", "seq")),
        check_vma=False,
    )
```
